256 devices in a mesh: dp: 16 (over x, y_hi, core), ctx: 16 (over z, y_lo).
Axes of the slice: x: 4, y: 4 (y_hi: 2, y_lo: 2; y = y_hi * 2 + y_lo), z: 8, core: 2. Of those that a mesh axis runs over, the one named last changes fastest.
Arguments:
- query_rows: bfloat16 [16, 2048, 2560], P('dp', 'ctx'), may hold values from -6 to 6
- key_rows: bfloat16 [16, 2048, 512], P('dp', 'ctx'), may hold values from -6 to 6
- value_rows: bfloat16 [16, 2048, 512], P('dp', 'ctx'), may hold values from -6 to 6
- forward_out: bfloat16 [16, 2048, 2560], P('dp', 'ctx'), may hold values from -6 to 6
- out_grad: bfloat16 [16, 2048, 2560], P('dp', 'ctx'), may hold values from -16 to 16
- lengths: int32 [16, 4], P('dp'), may hold values from 0 to 2048, as said below
- starts: int32 [16, 4], P('dp'), may hold values from 0 to 16, as said below
- adv_mask: int32 [16, 2048], P('dp', 'ctx'), may hold values from 0 to 1, as said below
Outputs:
- grad_query: bfloat16 [16, 2048, 2560], P('dp', 'ctx')
- grad_key: bfloat16 [16, 2048, 512], P('dp', 'ctx')
- grad_value: bfloat16 [16, 2048, 512], P('dp', 'ctx')
The draws below stay inside these ranges and needn't reach their ends.
Inputs may be any that keep to these rules, and one draw needn't show every extreme that they name: `lengths`: trace slot r of a row covers the shards from starts[r] up to the next slot's start (the last up to 16); its length is 0 where that span is empty and otherwise more than 128 times one less than the span and at most 128 times the span. Row 0 holds one trace of 2048 tokens. Each row's first slot starts at 0 and starts never fall along a row. `adv_mask`: the first token slot of every row is 1.
All inputs are finite; a program needn't handle non-finite values.
Results may differ from the reference program's by a relative error of at most 0.006.
Values may be sent and summed in bfloat16 or wider, within the bound.
No kernel may reach another device: no remote copies, remote signals or barrier semaphores. Data moves between devices by JAX's collectives and lax.ppermute only.
A program may use at most 64 MiB of HBM per device.

```python
import math
import jax
import jax.numpy as jnp
from jax import lax

KVH = 4
GROUP = 5
HD = 128
SHARD = 128
TRACES = 4
SHARDS = 16
ROWS = 16
TOKS = 2048


def spans_of(key):
    cuts = jnp.sort(jax.random.randint(jax.random.fold_in(key, 101), (ROWS, TRACES - 1), 0, SHARDS + 1), axis=1)
    cuts = cuts.at[0].set(SHARDS)
    first = jnp.concatenate([jnp.zeros((ROWS, 1), jnp.int32), cuts.astype(jnp.int32)], axis=1)
    ends = jnp.concatenate([cuts.astype(jnp.int32), jnp.full((ROWS, 1), SHARDS, jnp.int32)], axis=1)
    span = ends - first
    extra = jax.random.randint(jax.random.fold_in(key, 102), (ROWS, TRACES), 1, SHARD + 1)
    sizes_out = jnp.where(span > 0, (span - 1) * SHARD + extra, 0).astype(jnp.int32)
    sizes_out = sizes_out.at[0, 0].set(SHARDS * SHARD)
    return (first, sizes_out)


def draw_lengths(key, part):
    first, sizes_out = spans_of(key)
    return sizes_out


def draw_starts(key, part):
    first, sizes_out = spans_of(key)
    return first


def draw_adv_mask(key, part):
    key = jax.random.fold_in(key, 5)
    row_ids = jnp.arange(ROWS, dtype=jnp.int32)[:, None]
    chance = 20 + 60 * row_ids // max(ROWS - 1, 1)
    picks = jax.random.randint(key, (ROWS, TOKS), 0, 100)
    marks = (picks < chance).astype(jnp.int32)
    return marks.at[:, 0].set(1)


def draw_key_rows(key, part):
    key = jax.random.fold_in(key, 7)
    base = jnp.clip(jax.random.normal(key, (ROWS, SHARDS, SHARD, KVH, HD), jnp.float32), -6.0, 6.0)
    return base.reshape(ROWS, TOKS, KVH * HD).astype(jnp.bfloat16)


def draw_query_rows(key, part):
    key = jax.random.fold_in(key, 9)
    base = jnp.clip(jax.random.normal(key, (ROWS, SHARDS, SHARD, KVH, GROUP, HD), jnp.float32), -6.0, 6.0)
    return base.reshape(ROWS, TOKS, KVH * GROUP * HD).astype(jnp.bfloat16)


def block_scale(own_key, shape, cuts, smallest, top_value):
    def one(position, parts):
        draws = jax.random.uniform(jax.random.fold_in(jax.random.fold_in(own_key, 6), position), (parts,), jnp.float32, smallest / len(cuts), top_value / len(cuts))
        return jnp.repeat(jnp.exp(draws), shape[position] // parts).reshape((-1,) + (1,) * (len(shape) - position - 1))

    level = one(*cuts[0])
    for cut in cuts[1:]:
        level = level * one(*cut)
    return level


def normal_values(own_key, dims, width, reach, cuts=(), held_as=jnp.bfloat16):
    entries = jax.random.normal(own_key, dims, jnp.float32) * width
    if len(cuts) > 0:
        entries = block_scale(own_key, dims, cuts, -0.22, 0.18) * entries
    return jnp.clip(entries, min=-reach, max=reach).astype(held_as)


def setup_inputs(seed: int = 0) -> dict:
    seeds = jax.random.split(jax.random.key(seed), 9)
    query_rows = draw_query_rows(jax.random.fold_in(seeds[8], 71), 0)
    key_rows = draw_key_rows(jax.random.fold_in(seeds[8], 71), 0)
    value_rows = normal_values(seeds[2], (ROWS, TOKS, KVH * HD), 1.0, 6.0, ((0, 16), (1, 16)))
    forward_out = normal_values(seeds[3], (ROWS, TOKS, KVH * GROUP * HD), 1.0, 6.0, ((0, 16), (1, 16)))
    out_grad = normal_values(seeds[4], (ROWS, TOKS, KVH * GROUP * HD), 4.0, 16.0, ((0, 16), (1, 16)))
    lengths = draw_lengths(jax.random.fold_in(seeds[8], 71), 0)
    starts = draw_starts(jax.random.fold_in(seeds[8], 71), 0)
    adv_mask = draw_adv_mask(jax.random.fold_in(seeds[8], 71), 0)
    return {"query_rows": query_rows, "key_rows": key_rows, "value_rows": value_rows, "forward_out": forward_out, "out_grad": out_grad, "lengths": lengths, "starts": starts, "adv_mask": adv_mask}


def token_info(lengths_row, starts_row, tokens_at):
    begin = starts_row * SHARD
    inside = (tokens_at[None, :] >= begin[:, None]) & (tokens_at[None, :] < (begin + lengths_row)[:, None])
    trace_ids = jnp.arange(inside.shape[0], dtype=jnp.int32)[:, None]
    return (jnp.any(inside, axis=0), lax.optimization_barrier(jnp.sum(jnp.where(inside, trace_ids, 0), axis=0)).astype(jnp.int32))

def reference(query_rows, key_rows, value_rows, forward_out, out_grad, lengths, starts, adv_mask):
    inv_scale = 1.0 / math.sqrt(HD)
    positions = jnp.arange(TOKS, dtype=jnp.int32)
    live_all, doc_all = jax.vmap(lambda lens, firsts: token_info(lens, firsts, positions))(lengths, starts)
    used_all = adv_mask * live_all.astype(jnp.int32)
    scale = jnp.sum(live_all.astype(jnp.float32)) / jnp.sum(used_all.astype(jnp.float32))

    def one_row(items):
        queries, keys_in, values_in, outputs, grads, used_row, live, doc = items
        query_heads = queries.reshape(TOKS, KVH, GROUP, HD).astype(jnp.float32)
        key_heads = keys_in.reshape(TOKS, KVH, HD).astype(jnp.float32)
        value_heads = values_in.reshape(TOKS, KVH, HD).astype(jnp.float32)
        grad_in = lax.optimization_barrier((grads.astype(jnp.float32) * (used_row.astype(jnp.float32) * scale)[:, None]).astype(jnp.bfloat16))
        grad_heads = grad_in.reshape(TOKS, KVH, GROUP, HD).astype(jnp.float32)
        delta = lax.optimization_barrier(jnp.sum(grad_heads * outputs.reshape(TOKS, KVH, GROUP, HD).astype(jnp.float32), axis=-1)).transpose(1, 2, 0)
        allowed = live[:, None] & live[None, :] & (doc[:, None] == doc[None, :]) & (positions[None, :] <= positions[:, None])
        scores = jnp.einsum('tkgd,ukd->kgtu', query_heads, key_heads) * inv_scale
        run_max = lax.optimization_barrier(jnp.max(jnp.where(allowed, scores, -1e+30), axis=-1))
        sums = lax.optimization_barrier(jnp.sum(jnp.where(allowed, jnp.exp(scores - run_max[..., None]), 0.0), axis=-1))
        lse = jnp.where(live, run_max + jnp.log(jnp.where(live, sums, 1.0)), 0.0)
        prob = jnp.where(allowed, jnp.exp(scores - lse[..., None]), 0.0)
        prob_b = lax.optimization_barrier(prob.astype(jnp.bfloat16)).astype(jnp.float32)
        grad_v = jnp.einsum('kgtu,tkgd->ukd', prob_b, grad_heads)
        dprob = jnp.einsum('tkgd,ukd->kgtu', grad_heads, value_heads)
        dscore = lax.optimization_barrier((prob * (dprob - delta[..., None]) * inv_scale).astype(jnp.bfloat16)).astype(jnp.float32)
        grad_q = jnp.einsum('kgtu,ukd->tkgd', dscore, key_heads)
        grad_k = jnp.einsum('kgtu,tkgd->ukd', dscore, query_heads)
        return (grad_q.reshape(TOKS, KVH * GROUP * HD).astype(jnp.bfloat16), grad_k.reshape(TOKS, KVH * HD).astype(jnp.bfloat16), grad_v.reshape(TOKS, KVH * HD).astype(jnp.bfloat16))
    grad_query, grad_key, grad_value = lax.map(one_row, (query_rows, key_rows, value_rows, forward_out, out_grad, used_all, live_all, doc_all))
    return (grad_query, grad_key, grad_value)
```

```python
import functools
import math

import jax
import jax.numpy as jnp
from jax import lax
from jax.experimental import pallas as pl
from jax.experimental.pallas import tpu as pltpu
from jax.sharding import PartitionSpec as P

KVH = 4
GROUP = 5
HD = 128
SHARD = 128
RING = 8
HALF = KVH // 2
QH = HALF * GROUP
QROWS = QH * SHARD
UNIT = GROUP * SHARD
TAIL = 16
NEG = -1e30
BIG = 1e30
SCORE = math.log2(math.e) / math.sqrt(HD)
INV = 1.0 / math.sqrt(HD)
F32 = jnp.float32
BF16 = jnp.bfloat16
VMEM = pl.BlockSpec(memory_space=pltpu.VMEM)
SMEM = pl.BlockSpec(memory_space=pltpu.SMEM)
LIMIT = 48 * 1024 * 1024


def call(body, outs, ins, smem, flops=0, **kw):
    n = len(ins)
    return pl.pallas_call(
        body,
        out_shape=[jax.ShapeDtypeStruct(s, d) for s, d in outs],
        in_specs=[SMEM if i < smem else VMEM for i in range(n)],
        out_specs=[VMEM] * len(outs),
        compiler_params=pltpu.CompilerParams(vmem_limit_bytes=LIMIT),
        cost_estimate=pl.CostEstimate(flops=flops, bytes_accessed=4 << 20, transcendentals=0),
        **kw,
    )(*ins)


def prep_kernel(meta, len_ref, start_ref, adv, q, k, v, o, og, kv_keep, kv_send, q_keep, q_send, g_keep, g_send):
    z, y = meta[0], meta[1]
    shard = 2 * z + y
    tok = shard * SHARD + lax.broadcasted_iota(jnp.int32, (SHARD, SHARD), 1)
    live = jnp.zeros((SHARD, SHARD), F32)
    for r in range(4):
        begin = start_ref[0, r] * SHARD
        live = jnp.where((tok >= begin) & (tok < begin + len_ref[0, r]), 1.0, live)
    used = live * jnp.broadcast_to(adv[...], (SHARD, SHARD)).astype(F32)
    used_col = jnp.transpose(used)
    present = jnp.sum(live[:1], axis=1, keepdims=True)
    marked = jnp.sum(used[:1], axis=1, keepdims=True)
    lane = lax.broadcasted_iota(jnp.int32, (TAIL, 4 * HD), 1)
    counts = jnp.where(lane == 0, present, jnp.where(lane == 1, marked, 0.0)).astype(BF16)
    for mine, kv_out, q_out, g_out in ((True, kv_keep, q_keep, g_keep), (False, kv_send, q_send, g_send)):
        side = y if mine else 1 - y
        at = pl.multiple_of(side * (HALF * HD), HALF * HD)
        kv_out[:SHARD, : HALF * HD] = k[:, pl.ds(at, HALF * HD)]
        kv_out[:SHARD, HALF * HD :] = v[:, pl.ds(at, HALF * HD)]
        kv_out[SHARD:, :] = counts
        for h in range(QH):
            lanes = pl.ds(pl.multiple_of(side * (QH * HD) + h * HD, HD), HD)
            rows = slice(h * SHARD, (h + 1) * SHARD)
            q_out[rows, :] = q[:, lanes]
            grad = og[:, lanes].astype(F32) * used_col
            g_out[rows, :] = grad.astype(BF16)
            delta = jnp.sum(jnp.transpose(grad * o[:, lanes].astype(F32)), axis=0, keepdims=True)
            high = delta.astype(BF16)
            low = (delta - high.astype(F32)).astype(BF16)
            g_out[QROWS + h : QROWS + h + 1, :] = high
            g_out[QROWS + 16 + h : QROWS + 17 + h, :] = low


def begin_rows(len_ref, start_ref, shard):
    tok = shard * SHARD + lax.broadcasted_iota(jnp.int32, (1, SHARD), 1)
    first = jnp.full((1, SHARD), 1 << 20, jnp.int32)
    for r in range(4):
        begin = start_ref[0, r] * SHARD
        first = jnp.where((tok >= begin) & (tok < begin + len_ref[0, r]), start_ref[0, r], first)
    return first


def wide(row):
    return jnp.concatenate([row] * GROUP, axis=1)


def nt(a, b):
    return lax.dot_general(a, b, (((1,), (1,)), ((), ())), preferred_element_type=F32)


def tn(a, b):
    return lax.dot_general(a, b, (((0,), (0,)), ((), ())), preferred_element_type=F32)


def triangle():
    u = lax.broadcasted_iota(jnp.int32, (SHARD, SHARD), 0)
    t = lax.broadcasted_iota(jnp.int32, (SHARD, SHARD), 1)
    return wide(u <= t)


def sides(z, y):
    return (2 * z + y, 2 * z + 1 - y)


def total_step(kv_part, diagonal, key_z, z, y, len_ref, start_ref, queries, m_ref, l_ref):
    key_sides = sides(key_z, y)
    query_sides = sides(z, y)
    for src in range(2):
        first = begin_rows(len_ref, start_ref, query_sides[src])
        ok = [wide((first <= s) & (s <= query_sides[src])) for s in key_sides]
        for j in range(HALF):
            unit = src * HALF + j
            s = nt(kv_part[j], queries[src][j * UNIT : (j + 1) * UNIT, :]) * SCORE
            parts = [s[:SHARD], s[SHARD:]]
            if diagonal:
                parts[src] = jnp.where(triangle(), parts[src], NEG)
            m = m_ref[unit : unit + 1, :]
            new = m
            for part, good in zip(parts, ok):
                new = jnp.maximum(new, jnp.where(good, jnp.max(part, axis=0, keepdims=True), NEG))
            l = l_ref[unit : unit + 1, :] * jnp.exp2(m - new)
            for part, good in zip(parts, ok):
                l = l + jnp.sum(jnp.exp2(part - jnp.where(good, new, BIG)), axis=0, keepdims=True)
            m_ref[unit : unit + 1, :] = new
            l_ref[unit : unit + 1, :] = l


def keys_of(chunk):
    own, par = chunk
    take = lambda i: jnp.concatenate(
        [own[:SHARD, i * HD : (i + 1) * HD], par[:SHARD, i * HD : (i + 1) * HD]], axis=0
    )
    return [take(i) for i in range(HALF)], [take(HALF + i) for i in range(HALF)]


def halves(ref):
    return (ref.at[: SHARD + TAIL], ref.at[SHARD + TAIL :])


def counted(kvs):
    rows = (slice(SHARD, SHARD + TAIL), slice(2 * SHARD + TAIL, 2 * (SHARD + TAIL)))
    return sum(kv[r, :HD].astype(F32) for kv in kvs for r in rows)


def totals_kernel(first_call, offsets, *refs):
    meta, len_ref, start_ref, q_own, q_par = refs[:5]
    n = len(offsets)
    kvs = refs[5 : 5 + n]
    refs = refs[5 + n :]
    if not first_call:
        m_in, l_in, seen_in = refs[:3]
        refs = refs[3:]
    m_ref, l_ref, seen_ref = refs
    z, y = meta[0], meta[1]
    if first_call:
        m_ref[...] = jnp.full(m_ref.shape, NEG, F32)
        l_ref[...] = jnp.zeros(l_ref.shape, F32)
        seen = jnp.zeros(seen_ref.shape, F32)
    else:
        m_ref[...] = m_in[...]
        l_ref[...] = l_in[...]
        seen = seen_in[...]
    seen_ref[...] = seen + counted(kvs)
    for offset, kv in zip(offsets, kvs):

        @pl.when(z >= offset)
        def _():
            keys, _ = keys_of(halves(kv))
            total_step(keys, offset == 0, z - offset, z, y, len_ref, start_ref, (q_own, q_par), m_ref, l_ref)


def grads_kernel(offsets, last_total, first_call, final, *refs):
    meta, len_ref, start_ref, q_own, q_par, g_own, g_par = refs[:7]
    refs = refs[7:]
    n = len(offsets)
    kvs = refs[:n]
    refs = refs[n:]
    if first_call:
        m_in, l_in, seen_in = refs[:3]
        refs = refs[3:]
    else:
        lse_in, dq_in = refs[:2]
        refs = refs[2:]
    parts = refs[:n]
    refs = refs[n:]
    if first_call:
        lse_ref, dq_ref, seen_ref, m_ref, l_ref = refs
    elif final:
        dq_own, dq_par, dq_ref = refs
        lse_ref = lse_in
    else:
        (dq_ref,) = refs
        lse_ref = lse_in
    z, y = meta[0], meta[1]
    queries, grads = (q_own, q_par), (g_own, g_par)
    query_sides = sides(z, y)
    if first_call:
        m_ref[...] = m_in[...]
        l_ref[...] = l_in[...]
        seen_ref[...] = seen_in[...] + counted(kvs[:1])

        @pl.when(z >= last_total)
        def _():
            keys, _ = keys_of(halves(kvs[0]))
            total_step(keys, False, z - last_total, z, y, len_ref, start_ref, queries, m_ref, l_ref)

        total = l_ref[...]
        lse_ref[...] = jnp.where(total > 0.0, m_ref[...] + jnp.log2(jnp.where(total > 0.0, total, 1.0)), BIG)
        dq_ref[...] = jnp.zeros(dq_ref.shape, F32)
    else:
        dq_ref[...] = dq_in[...]
    for offset, kv, part in zip(offsets, kvs, parts):

        @pl.when(z < offset)
        def _():
            part[...] = jnp.zeros(part.shape, part.dtype)

        @pl.when(z >= offset)
        def _():
            keys, values = keys_of(halves(kv))
            key_sides = sides(z - offset, y)
            for j in range(HALF):
                grad_k = jnp.zeros((2 * SHARD, HD), F32)
                grad_v = jnp.zeros((2 * SHARD, HD), F32)
                for src in range(2):
                    unit = src * HALF + j
                    rows = slice(j * UNIT, (j + 1) * UNIT)
                    first = begin_rows(len_ref, start_ref, query_sides[src])
                    lse = lse_ref[unit : unit + 1, :]
                    query = queries[src][rows, :]
                    grad = grads[src][rows, :]
                    heads = range(j * GROUP, (j + 1) * GROUP)
                    delta = jnp.concatenate(
                        [
                            grads[src][QROWS + h : QROWS + h + 1, :].astype(F32)
                            + grads[src][QROWS + 16 + h : QROWS + 17 + h, :].astype(F32)
                            for h in heads
                        ],
                        axis=1,
                    )
                    s = nt(keys[j], query) * SCORE
                    probs = []
                    for half in range(2):
                        good = wide((first <= key_sides[half]) & (key_sides[half] <= query_sides[src]))
                        p = jnp.exp2(s[half * SHARD : (half + 1) * SHARD] - jnp.where(good, lse, BIG))
                        if offset == 0 and half == src:
                            p = jnp.where(triangle(), p, 0.0)
                        probs.append(p)
                    prob = jnp.concatenate(probs, axis=0)
                    grad_v = grad_v + jnp.dot(prob.astype(BF16), grad, preferred_element_type=F32)
                    dscore = (prob * (nt(values[j], grad) - delta)).astype(BF16)
                    grad_k = grad_k + jnp.dot(dscore, query, preferred_element_type=F32)
                    dq_ref[unit] += tn(keys[j], dscore)
                part[:, j * HD : (j + 1) * HD] = (grad_k * INV).astype(part.dtype)
                part[:, (HALF + j) * HD : (HALF + j + 1) * HD] = grad_v.astype(part.dtype)

    if final:
        for src, out in enumerate((dq_own, dq_par)):
            for h in range(QH):
                j, g = divmod(h, GROUP)
                block = dq_ref[src * HALF + j, :, g * SHARD : (g + 1) * SHARD]
                out[:, h * HD : (h + 1) * HD] = (jnp.transpose(block) * INV).astype(BF16)


def finish_kernel(meta, dq_own, dq_back, kv_own, kv_back, seen, grad_query, grad_key, grad_value):
    y = meta[1]
    scale = jnp.broadcast_to(seen[:1, 0:1] / seen[:1, 1:2], (1, HD))
    for mine, dq, kv in ((True, dq_own, kv_own), (False, dq_back, kv_back)):
        side = y if mine else 1 - y
        for h in range(QH):
            lanes = pl.ds(pl.multiple_of(side * (QH * HD) + h * HD, HD), HD)
            grad_query[:, lanes] = (dq[:, h * HD : (h + 1) * HD].astype(F32) * scale).astype(BF16)
        for j in range(HALF):
            lanes = pl.ds(pl.multiple_of((side * HALF + j) * HD, HD), HD)
            grad_key[:, lanes] = (kv[:, j * HD : (j + 1) * HD].astype(F32) * scale).astype(BF16)
            value = kv[:, (HALF + j) * HD : (HALF + j + 1) * HD].astype(F32) * scale
            grad_value[:, lanes] = value.astype(BF16)


def per_device(query_rows, key_rows, value_rows, forward_out, out_grad, lengths, starts, adv_mask):
    here = lax.axis_index("ctx")
    z, y = here // 2, here % 2
    meta = jnp.stack([z, y]).astype(jnp.int32)
    rows_dp = lax.axis_size("dp")

    def along(value, steps, sources):
        pairs = [(2 * s + w, 2 * ((s + steps) % RING) + w) for s in sources for w in range(2)]
        return lax.ppermute(value, "ctx", pairs)

    def across(value):
        return lax.ppermute(value, "ctx", [(i, i ^ 1) for i in range(2 * RING)])

    scalars = (meta, lengths, starts)
    kv_shape = ((SHARD + TAIL, 4 * HD), BF16)
    q_shape = ((QROWS, HD), BF16)
    g_shape = ((QROWS + 32, HD), BF16)
    kv_keep, kv_send, q_own, q_send, g_own, g_send = call(
        prep_kernel,
        [kv_shape, kv_shape, q_shape, q_shape, g_shape, g_shape],
        (*scalars, adv_mask, query_rows[0], key_rows[0], value_rows[0], forward_out[0], out_grad[0]),
        3,
        flops=1 << 28,
    )
    kv_own = jnp.concatenate([kv_keep, across(kv_send)], axis=0)
    q_par = across(q_send)
    g_par = across(g_send)

    held = {0: kv_own}
    ahead = back = kv_own
    for s in range(1, 5):
        ahead = along(ahead, 1, range(RING))
        held[s] = ahead
        if s < 4:
            back = along(back, -1, range(RING))
            held[RING - s] = back

    state = [((2 * HALF, UNIT), F32)] * 2 + [((TAIL, HD), F32)]
    unit_flops = 2 * 256 * UNIT * HD * 4

    def totals(offsets, prev):
        return call(
            functools.partial(totals_kernel, prev is None, offsets),
            state,
            (*scalars, q_own, q_par, *[held[i] for i in offsets], *(prev or ())),
            3,
            flops=4 * unit_flops * len(offsets),
        )

    ml = totals((0,), None)
    ml = totals((1, 7), ml)
    ml = totals((2, 6), ml)
    ml = totals((3, 5), ml)

    dq_shape = ((2 * HALF, HD, UNIT), F32)
    part_shape = (2 * SHARD, 4 * HD)
    common = (*scalars, q_own, q_par, g_own, g_par)

    def grads(offsets, extra, outs, first_call=False, final=False, kind=F32, **kw):
        return call(
            functools.partial(grads_kernel, offsets, 4, first_call, final),
            [(part_shape, kind)] * len(offsets) + outs,
            (*common, *[held[i] for i in offsets], *extra),
            3,
            flops=8 * unit_flops * len(offsets),
            **kw,
        )

    part4, part5, lse, dq, seen = grads(
        (4, 5),
        ml,
        [((2 * HALF, UNIT), F32), dq_shape, ((TAIL, HD), F32)],
        first_call=True,
        kind=BF16,
        scratch_shapes=[pltpu.VMEM((2 * HALF, UNIT), F32)] * 2,
    )
    part3, part6, dq = grads((3, 6), (lse, dq), [dq_shape])
    part2, part7, dq = grads((2, 7), (lse, dq), [dq_shape])
    part1, part0, dq_own, dq_par = grads(
        (1, 0),
        (lse, dq),
        [((SHARD, QH * HD), BF16)] * 2,
        final=True,
        scratch_shapes=[pltpu.VMEM(*dq_shape)],
    )

    def add(moved, part):
        return (moved.astype(F32) + part).astype(BF16)

    down = along(part4, -1, range(4, 8))
    up = along(part5, 1, (5, 6, 7))
    down = along(add(down, part3), -1, range(3, 8))
    up = along(add(up, part6), 1, (6, 7, 0))
    down = along(add(down, part2), -1, range(2, 8))
    up = along(add(up, part7), 1, (7, 0, 1))
    down = along(add(down, part1), -1, range(1, 8))
    dq_back = across(dq_par)

    total = part0 + down.astype(F32) + up.astype(F32)
    kv_back = across(total[SHARD:].astype(BF16))
    for bit in (1, 2, 4, 8):
        if bit < rows_dp:
            seen = seen + lax.ppermute(seen, "dp", [(i, i ^ bit) for i in range(rows_dp)])
    grad_query, grad_key, grad_value = call(
        finish_kernel,
        [((SHARD, KVH * GROUP * HD), BF16), ((SHARD, KVH * HD), BF16), ((SHARD, KVH * HD), BF16)],
        (meta, dq_own, dq_back, total[:SHARD], kv_back, seen),
        1,
    )
    return grad_query[None], grad_key[None], grad_value[None]


def solution(mesh):
    in_specs = (
        P("dp", "ctx", None),
        P("dp", "ctx", None),
        P("dp", "ctx", None),
        P("dp", "ctx", None),
        P("dp", "ctx", None),
        P("dp", None),
        P("dp", None),
        P("dp", "ctx"),
    )
    out_specs = (P("dp", "ctx", None), P("dp", "ctx", None), P("dp", "ctx", None))
    return jax.shard_map(
        per_device, mesh=mesh, in_specs=in_specs, out_specs=out_specs, check_vma=False
    )
```

```python
import functools
import math

import jax
import jax.numpy as jnp
from jax import lax
from jax.experimental import pallas as pl
from jax.experimental.pallas import tpu as pltpu
from jax.sharding import PartitionSpec as P

KVH = 4
GROUP = 5
HD = 128
SHARD = 128
RING = 8
HALF = KVH // 2
QH = HALF * GROUP
QROWS = QH * SHARD
UNIT = GROUP * SHARD
TAIL = 16
NEG = -1e30
BIG = 1e30
SCORE = math.log2(math.e) / math.sqrt(HD)
INV = 1.0 / math.sqrt(HD)
F32 = jnp.float32
BF16 = jnp.bfloat16
VMEM = pl.BlockSpec(memory_space=pltpu.VMEM)
SMEM = pl.BlockSpec(memory_space=pltpu.SMEM)
HBM = pl.BlockSpec(memory_space=pltpu.HBM)
DEAD = 1 << 20
LIMIT = 48 * 1024 * 1024


def call(body, outs, ins, specs, flops=0, **kw):
    return pl.pallas_call(
        body,
        out_shape=[jax.ShapeDtypeStruct(s, d) for s, d in outs],
        in_specs=list(specs) + [VMEM] * (len(ins) - len(specs)),
        out_specs=[VMEM] * len(outs),
        compiler_params=pltpu.CompilerParams(vmem_limit_bytes=LIMIT),
        cost_estimate=pl.CostEstimate(flops=flops, bytes_accessed=4 << 20, transcendentals=0),
        **kw,
    )(*ins)


def in_hbm(value):
    return pltpu.with_memory_space_constraint(value, pltpu.HBM)


def fetch(copies, sems):
    started = [pltpu.make_async_copy(a, b, sems.at[i]) for i, (a, b) in enumerate(copies)]
    for one in started:
        one.start()
    return started


def half_lanes(side, width):
    return pl.ds(pl.multiple_of(side * width, width), width)


def keys_kernel(meta, len_hbm, start_hbm, adv_hbm, k, v, kv_keep, kv_send, first_ref, used_ref, lens, begins, adv, sems):
    z, y = meta[0], meta[1]
    width = HALF * HD
    copies = [(len_hbm, lens), (start_hbm, begins), (adv_hbm, adv)]
    for side, out in ((y, kv_keep), (1 - y, kv_send)):
        copies.append((k.at[:, half_lanes(side, width)], out.at[:SHARD, :width]))
        copies.append((v.at[:, half_lanes(side, width)], out.at[:SHARD, width:]))
    started = fetch(copies, sems)
    for one in started[:3]:
        one.wait()
    for i, shard in enumerate(sides(z, y)):
        tok = shard * SHARD + lax.broadcasted_iota(jnp.int32, (1, SHARD), 1)
        first = jnp.full((1, SHARD), DEAD, jnp.int32)
        for r in range(4):
            begin = begins[0, r] * SHARD
            first = jnp.where((tok >= begin) & (tok < begin + lens[0, r]), begins[0, r], first)
        first_ref[i : i + 1, :] = first
    live = (first_ref[:1, :] < DEAD).astype(F32)
    used = live * adv[...].astype(F32)
    used_ref[...] = jnp.broadcast_to(used, used_ref.shape)
    present = jnp.sum(live, axis=1, keepdims=True)
    marked = jnp.sum(used, axis=1, keepdims=True)
    lane = lax.broadcasted_iota(jnp.int32, (TAIL, 4 * HD), 1)
    counts = jnp.where(lane == 0, present, jnp.where(lane == 1, marked, 0.0)).astype(BF16)
    kv_keep[SHARD:, :] = counts
    kv_send[SHARD:, :] = counts
    for one in started[3:]:
        one.wait()


def queries_kernel(meta, used, q, o, og, q_keep, q_send, g_keep, g_send, q_buf, o_buf, og_buf, sems):
    y = meta[1]
    width = QH * HD
    copies = []
    for i, side in ((1, 1 - y), (0, y)):
        for whole, buf in ((q, q_buf), (og, og_buf), (o, o_buf)):
            copies.append((whole.at[:, half_lanes(side, width)], buf.at[i]))
    started = fetch(copies, sems)
    used_col = jnp.transpose(jnp.broadcast_to(used[:1, :], (SHARD, SHARD)))
    for n, (i, q_out, g_out) in enumerate(((1, q_send, g_send), (0, q_keep, g_keep))):
        for one in started[3 * n : 3 * n + 3]:
            one.wait()
        for h in range(QH):
            lanes = slice(h * HD, (h + 1) * HD)
            rows = slice(h * SHARD, (h + 1) * SHARD)
            q_out[rows, :] = q_buf[i, :, lanes]
            grad = og_buf[i, :, lanes].astype(F32) * used_col
            g_out[rows, :] = grad.astype(BF16)
            delta = jnp.sum(jnp.transpose(grad * o_buf[i, :, lanes].astype(F32)), axis=0, keepdims=True)
            high = delta.astype(BF16)
            low = (delta - high.astype(F32)).astype(BF16)
            g_out[QROWS + h : QROWS + h + 1, :] = high
            g_out[QROWS + 16 + h : QROWS + 17 + h, :] = low


def wide(row):
    return jnp.concatenate([row] * GROUP, axis=1)


def nt(a, b):
    return lax.dot_general(a, b, (((1,), (1,)), ((), ())), preferred_element_type=F32)


def tn(a, b):
    return lax.dot_general(a, b, (((0,), (0,)), ((), ())), preferred_element_type=F32)


def triangle():
    u = lax.broadcasted_iota(jnp.int32, (SHARD, SHARD), 0)
    t = lax.broadcasted_iota(jnp.int32, (SHARD, SHARD), 1)
    return wide(u <= t)


def sides(z, y):
    return (2 * z + y, 2 * z + 1 - y)


def total_step(kv_part, diagonal, key_z, z, y, first_ref, queries, m_ref, l_ref):
    key_sides = sides(key_z, y)
    query_sides = sides(z, y)
    for src in range(2):
        first = first_ref[src : src + 1, :]
        ok = [wide((first <= s) & (s <= query_sides[src])) for s in key_sides]
        for j in range(HALF):
            unit = src * HALF + j
            s = nt(kv_part[j], queries[src][j * UNIT : (j + 1) * UNIT, :]) * SCORE
            parts = [s[:SHARD], s[SHARD:]]
            if diagonal:
                parts[src] = jnp.where(triangle(), parts[src], NEG)
            m = m_ref[unit : unit + 1, :]
            new = m
            for part, good in zip(parts, ok):
                new = jnp.maximum(new, jnp.where(good, jnp.max(part, axis=0, keepdims=True), NEG))
            l = l_ref[unit : unit + 1, :] * jnp.exp2(m - new)
            for part, good in zip(parts, ok):
                l = l + jnp.sum(jnp.exp2(part - jnp.where(good, new, BIG)), axis=0, keepdims=True)
            m_ref[unit : unit + 1, :] = new
            l_ref[unit : unit + 1, :] = l


def keys_of(chunk):
    own, par = chunk
    take = lambda i: jnp.concatenate(
        [own[:SHARD, i * HD : (i + 1) * HD], par[:SHARD, i * HD : (i + 1) * HD]], axis=0
    )
    return [take(i) for i in range(HALF)], [take(HALF + i) for i in range(HALF)]


def halves(ref):
    return (ref.at[: SHARD + TAIL], ref.at[SHARD + TAIL :])


def counted(kvs):
    rows = (slice(SHARD, SHARD + TAIL), slice(2 * SHARD + TAIL, 2 * (SHARD + TAIL)))
    return sum(kv[r, :HD].astype(F32) for kv in kvs for r in rows)


def totals_kernel(first_call, offsets, *refs):
    meta, first_ref, q_own, q_par = refs[:4]
    n = len(offsets)
    kvs = refs[4 : 4 + n]
    refs = refs[4 + n :]
    if not first_call:
        m_in, l_in, seen_in = refs[:3]
        refs = refs[3:]
    m_ref, l_ref, seen_ref = refs
    z, y = meta[0], meta[1]
    if first_call:
        m_ref[...] = jnp.full(m_ref.shape, NEG, F32)
        l_ref[...] = jnp.zeros(l_ref.shape, F32)
        seen = jnp.zeros(seen_ref.shape, F32)
    else:
        m_ref[...] = m_in[...]
        l_ref[...] = l_in[...]
        seen = seen_in[...]
    seen_ref[...] = seen + counted(kvs)
    for offset, kv in zip(offsets, kvs):

        @pl.when(z >= offset)
        def _():
            keys, _ = keys_of(halves(kv))
            total_step(keys, offset == 0, z - offset, z, y, first_ref, (q_own, q_par), m_ref, l_ref)


def grads_kernel(offsets, last_total, first_call, final, *refs):
    meta, first_ref, q_own, q_par, g_own, g_par = refs[:6]
    refs = refs[6:]
    n = len(offsets)
    kvs = refs[:n]
    refs = refs[n:]
    if first_call:
        m_in, l_in, seen_in = refs[:3]
        refs = refs[3:]
    else:
        lse_in, dq_in = refs[:2]
        refs = refs[2:]
    parts = refs[:n]
    refs = refs[n:]
    if first_call:
        lse_ref, dq_ref, seen_ref, m_ref, l_ref = refs
    elif final:
        dq_own, dq_par, dq_ref = refs
        lse_ref = lse_in
    else:
        (dq_ref,) = refs
        lse_ref = lse_in
    z, y = meta[0], meta[1]
    queries, grads = (q_own, q_par), (g_own, g_par)
    query_sides = sides(z, y)
    if first_call:
        m_ref[...] = m_in[...]
        l_ref[...] = l_in[...]
        seen_ref[...] = seen_in[...] + counted(kvs[:1])

        @pl.when(z >= last_total)
        def _():
            keys, _ = keys_of(halves(kvs[0]))
            total_step(keys, False, z - last_total, z, y, first_ref, queries, m_ref, l_ref)

        total = l_ref[...]
        lse_ref[...] = jnp.where(total > 0.0, m_ref[...] + jnp.log2(jnp.where(total > 0.0, total, 1.0)), BIG)
        dq_ref[...] = jnp.zeros(dq_ref.shape, F32)
    else:
        dq_ref[...] = dq_in[...]
    for offset, kv, part in zip(offsets, kvs, parts):

        @pl.when(z < offset)
        def _():
            part[...] = jnp.zeros(part.shape, part.dtype)

        @pl.when(z >= offset)
        def _():
            keys, values = keys_of(halves(kv))
            key_sides = sides(z - offset, y)
            for j in range(HALF):
                grad_k = jnp.zeros((2 * SHARD, HD), F32)
                grad_v = jnp.zeros((2 * SHARD, HD), F32)
                for src in range(2):
                    unit = src * HALF + j
                    rows = slice(j * UNIT, (j + 1) * UNIT)
                    first = first_ref[src : src + 1, :]
                    lse = lse_ref[unit : unit + 1, :]
                    query = queries[src][rows, :]
                    grad = grads[src][rows, :]
                    heads = range(j * GROUP, (j + 1) * GROUP)
                    delta = jnp.concatenate(
                        [
                            grads[src][QROWS + h : QROWS + h + 1, :].astype(F32)
                            + grads[src][QROWS + 16 + h : QROWS + 17 + h, :].astype(F32)
                            for h in heads
                        ],
                        axis=1,
                    )
                    s = nt(keys[j], query) * SCORE
                    probs = []
                    for half in range(2):
                        good = wide((first <= key_sides[half]) & (key_sides[half] <= query_sides[src]))
                        p = jnp.exp2(s[half * SHARD : (half + 1) * SHARD] - jnp.where(good, lse, BIG))
                        if offset == 0 and half == src:
                            p = jnp.where(triangle(), p, 0.0)
                        probs.append(p)
                    prob = jnp.concatenate(probs, axis=0)
                    grad_v = grad_v + jnp.dot(prob.astype(BF16), grad, preferred_element_type=F32)
                    dscore = (prob * (nt(values[j], grad) - delta)).astype(BF16)
                    grad_k = grad_k + jnp.dot(dscore, query, preferred_element_type=F32)
                    dq_ref[unit] += tn(keys[j], dscore)
                part[:, j * HD : (j + 1) * HD] = (grad_k * INV).astype(part.dtype)
                part[:, (HALF + j) * HD : (HALF + j + 1) * HD] = grad_v.astype(part.dtype)

    if final:
        for src, out in enumerate((dq_own, dq_par)):
            for h in range(QH):
                j, g = divmod(h, GROUP)
                block = dq_ref[src * HALF + j, :, g * SHARD : (g + 1) * SHARD]
                out[:, h * HD : (h + 1) * HD] = (jnp.transpose(block) * INV).astype(BF16)


def finish_kernel(meta, dq_own, dq_back, kv_own, kv_back, seen, grad_query, grad_key, grad_value):
    y = meta[1]
    scale = jnp.broadcast_to(seen[:1, 0:1] / seen[:1, 1:2], (1, HD))
    for mine, dq, kv in ((True, dq_own, kv_own), (False, dq_back, kv_back)):
        side = y if mine else 1 - y
        for h in range(QH):
            lanes = pl.ds(pl.multiple_of(side * (QH * HD) + h * HD, HD), HD)
            grad_query[:, lanes] = (dq[:, h * HD : (h + 1) * HD].astype(F32) * scale).astype(BF16)
        for j in range(HALF):
            lanes = pl.ds(pl.multiple_of((side * HALF + j) * HD, HD), HD)
            grad_key[:, lanes] = (kv[:, j * HD : (j + 1) * HD].astype(F32) * scale).astype(BF16)
            value = kv[:, (HALF + j) * HD : (HALF + j + 1) * HD].astype(F32) * scale
            grad_value[:, lanes] = value.astype(BF16)


def per_device(query_rows, key_rows, value_rows, forward_out, out_grad, lengths, starts, adv_mask):
    here = lax.axis_index("ctx")
    z, y = here // 2, here % 2
    meta = jnp.stack([z, y]).astype(jnp.int32)
    rows_dp = lax.axis_size("dp")

    def along(value, steps, sources, flip=0):
        pairs = [(2 * s + w, 2 * ((s + steps) % RING) + (w ^ flip)) for s in sources for w in range(2)]
        return lax.ppermute(value, "ctx", pairs)

    def across(value):
        return lax.ppermute(value, "ctx", [(i, i ^ 1) for i in range(2 * RING)])

    kv_shape = ((SHARD + TAIL, 4 * HD), BF16)
    q_shape = ((QROWS, HD), BF16)
    g_shape = ((QROWS + 32, HD), BF16)
    kv_keep, kv_send, first, used = call(
        keys_kernel,
        [kv_shape, kv_shape, ((8, SHARD), jnp.int32), ((8, SHARD), F32)],
        (meta, *map(in_hbm, (lengths, starts, adv_mask, key_rows[0], value_rows[0]))),
        [SMEM] + [HBM] * 5,
        scratch_shapes=[
            pltpu.SMEM((1, 4), jnp.int32),
            pltpu.SMEM((1, 4), jnp.int32),
            pltpu.VMEM((1, SHARD), jnp.int32),
            pltpu.SemaphoreType.DMA((7,)),
        ],
    )
    q_own, q_send, g_own, g_send = call(
        queries_kernel,
        [q_shape, q_shape, g_shape, g_shape],
        (meta, used, *map(in_hbm, (query_rows[0], forward_out[0], out_grad[0]))),
        [SMEM, VMEM] + [HBM] * 3,
        flops=1 << 28,
        scratch_shapes=[pltpu.VMEM((2, SHARD, QH * HD), BF16)] * 3 + [pltpu.SemaphoreType.DMA((6,))],
    )

    everyone = range(RING)
    ahead = jnp.concatenate([along(kv_keep, 1, everyone), along(kv_send, 1, everyone, 1)], axis=0)
    back = jnp.concatenate([along(kv_keep, -1, everyone), along(kv_send, -1, everyone, 1)], axis=0)
    held = {0: jnp.concatenate([kv_keep, across(kv_send)], axis=0), 1: ahead, RING - 1: back}
    q_par = across(q_send)
    g_par = across(g_send)
    for s in (2, 3):
        held[s] = ahead = along(ahead, 1, everyone)
        held[RING - s] = back = along(back, -1, everyone)

    state = [((2 * HALF, UNIT), F32)] * 2 + [((TAIL, HD), F32)]
    unit_flops = 2 * 256 * UNIT * HD * 4

    def totals(offsets, prev):
        return call(
            functools.partial(totals_kernel, prev is None, offsets),
            state,
            (meta, first, q_own, q_par, *[held[i] for i in offsets], *(prev or ())),
            [SMEM],
            flops=4 * unit_flops * len(offsets),
        )

    ml = totals((0,), None)
    ml = totals((1, 7), ml)
    ml = totals((2, 6), ml)
    ahead, ml = lax.optimization_barrier((ahead, ml))
    held[4] = along(ahead, 1, everyone)
    ml = totals((3, 5), ml)

    dq_shape = ((2 * HALF, HD, UNIT), F32)
    part_shape = (2 * SHARD, 4 * HD)
    common = (meta, first, q_own, q_par, g_own, g_par)

    def grads(offsets, extra, outs, first_call=False, final=False, kind=F32, **kw):
        return call(
            functools.partial(grads_kernel, offsets, 4, first_call, final),
            [(part_shape, kind)] * len(offsets) + outs,
            (*common, *[held[i] for i in offsets], *extra),
            [SMEM],
            flops=8 * unit_flops * len(offsets),
            **kw,
        )

    part4, part5, lse, dq, seen = grads(
        (4, 5),
        ml,
        [((2 * HALF, UNIT), F32), dq_shape, ((TAIL, HD), F32)],
        first_call=True,
        kind=BF16,
        scratch_shapes=[pltpu.VMEM((2 * HALF, UNIT), F32)] * 2,
    )
    part3, part6, dq = grads((3, 6), (lse, dq), [dq_shape])
    part2, part7, dq = grads((2, 7), (lse, dq), [dq_shape])
    part1, part0, dq_own, dq_par = grads(
        (1, 0),
        (lse, dq),
        [((SHARD, QH * HD), BF16)] * 2,
        final=True,
        scratch_shapes=[pltpu.VMEM(*dq_shape)],
    )

    def add(moved, part):
        return (moved.astype(F32) + part).astype(BF16)

    def seen_step(seen, bit):
        if bit >= rows_dp:
            return seen
        return seen + lax.ppermute(seen, "dp", [(i, i ^ bit) for i in range(rows_dp)])

    down = along(part4, -1, range(4, 8))
    up = along(part5, 1, (5, 6, 7))
    seen = seen_step(seen, 1)
    down, seen = lax.optimization_barrier((add(down, part3), seen))
    down = along(down, -1, range(3, 8))
    up = along(add(up, part6), 1, (6, 7, 0))
    seen = seen_step(seen, 2)
    down, seen = lax.optimization_barrier((add(down, part2), seen))
    down = along(down, -1, range(2, 8))
    up = along(add(up, part7), 1, (7, 0, 1))
    seen = seen_step(seen, 4)
    down, seen = lax.optimization_barrier((add(down, part1), seen))
    down = along(down, -1, range(1, 8))
    dq_back = across(dq_par)
    seen = seen_step(seen, 8)
    total = part0 + down.astype(F32) + up.astype(F32)
    kv_back = across(total[SHARD:].astype(BF16))
    grad_query, grad_key, grad_value = call(
        finish_kernel,
        [((SHARD, KVH * GROUP * HD), BF16), ((SHARD, KVH * HD), BF16), ((SHARD, KVH * HD), BF16)],
        (meta, dq_own, dq_back, total[:SHARD], kv_back, seen),
        [SMEM],
    )
    return grad_query[None], grad_key[None], grad_value[None]


def solution(mesh):
    in_specs = (
        P("dp", "ctx", None),
        P("dp", "ctx", None),
        P("dp", "ctx", None),
        P("dp", "ctx", None),
        P("dp", "ctx", None),
        P("dp", None),
        P("dp", None),
        P("dp", "ctx"),
    )
    out_specs = (P("dp", "ctx", None), P("dp", "ctx", None), P("dp", "ctx", None))
    return jax.shard_map(
        per_device, mesh=mesh, in_specs=in_specs, out_specs=out_specs, check_vma=False
    )
```

```python
import functools
import math

import jax
import jax.numpy as jnp
from jax import lax
from jax.experimental import pallas as pl
from jax.experimental.pallas import tpu as pltpu
from jax.sharding import PartitionSpec as P

KVH = 4
GROUP = 5
HD = 128
SHARD = 128
RING = 8
HALF = KVH // 2
QH = HALF * GROUP
QROWS = QH * SHARD
UNIT = GROUP * SHARD
TAIL = 16
NEG = -1e30
BIG = 1e30
SCORE = math.log2(math.e) / math.sqrt(HD)
INV = 1.0 / math.sqrt(HD)
F32 = jnp.float32
BF16 = jnp.bfloat16
VMEM = pl.BlockSpec(memory_space=pltpu.VMEM)
SMEM = pl.BlockSpec(memory_space=pltpu.SMEM)
HBM = pl.BlockSpec(memory_space=pltpu.HBM)
DEAD = 1 << 20
LIMIT = 48 * 1024 * 1024


def call(body, outs, ins, specs, flops=0, **kw):
    return pl.pallas_call(
        body,
        out_shape=[jax.ShapeDtypeStruct(s, d) for s, d in outs],
        in_specs=list(specs) + [VMEM] * (len(ins) - len(specs)),
        out_specs=[VMEM] * len(outs),
        compiler_params=pltpu.CompilerParams(vmem_limit_bytes=LIMIT),
        cost_estimate=pl.CostEstimate(flops=flops, bytes_accessed=4 << 20, transcendentals=0),
        **kw,
    )(*ins)


def in_hbm(value):
    return pltpu.with_memory_space_constraint(value, pltpu.HBM)


def fetch(copies, sems):
    started = [pltpu.make_async_copy(a, b, sems.at[i]) for i, (a, b) in enumerate(copies)]
    for one in started:
        one.start()
    return started


def half_lanes(side, width):
    return pl.ds(pl.multiple_of(side * width, width), width)


def keys_kernel(meta, len_hbm, start_hbm, adv_hbm, k, v, kv_keep, kv_send, first_ref, used_ref, count_ref, lens, begins, adv, sems):
    z, y = meta[0], meta[1]
    width = HALF * HD
    copies = [(len_hbm, lens), (start_hbm, begins), (adv_hbm, adv)]
    for side, out in ((y, kv_keep), (1 - y, kv_send)):
        copies.append((k.at[:, half_lanes(side, width)], out.at[:, :width]))
        copies.append((v.at[:, half_lanes(side, width)], out.at[:, width:]))
    started = fetch(copies, sems)
    for one in started[:3]:
        one.wait()
    for i, shard in enumerate(sides(z, y)):
        tok = shard * SHARD + lax.broadcasted_iota(jnp.int32, (1, SHARD), 1)
        first = jnp.full((1, SHARD), DEAD, jnp.int32)
        for r in range(4):
            begin = begins[0, r] * SHARD
            first = jnp.where((tok >= begin) & (tok < begin + lens[0, r]), begins[0, r], first)
        first_ref[i : i + 1, :] = first
    live = (first_ref[:1, :] < DEAD).astype(F32)
    used = live * adv[...].astype(F32)
    used_ref[...] = jnp.broadcast_to(used, used_ref.shape)
    present = jnp.sum(live, axis=1, keepdims=True)
    marked = jnp.sum(used, axis=1, keepdims=True)
    lane = lax.broadcasted_iota(jnp.int32, count_ref.shape, 1)
    count_ref[...] = jnp.where(lane == 0, present, jnp.where(lane == 1, marked, 0.0))
    for one in started[3:]:
        one.wait()


def queries_kernel(meta, used, q, o, og, q_keep, q_send, g_keep, g_send, q_buf, o_buf, og_buf, sems):
    y = meta[1]
    width = QH * HD
    copies = []
    for i, side in ((1, 1 - y), (0, y)):
        for whole, buf in ((q, q_buf), (og, og_buf), (o, o_buf)):
            copies.append((whole.at[:, half_lanes(side, width)], buf.at[i]))
    started = fetch(copies, sems)
    used_col = jnp.transpose(jnp.broadcast_to(used[:1, :], (SHARD, SHARD)))
    for n, (i, q_out, g_out) in enumerate(((1, q_send, g_send), (0, q_keep, g_keep))):
        for one in started[3 * n : 3 * n + 3]:
            one.wait()
        for h in range(QH):
            lanes = slice(h * HD, (h + 1) * HD)
            rows = slice(h * SHARD, (h + 1) * SHARD)
            q_out[rows, :] = q_buf[i, :, lanes]
            grad = og_buf[i, :, lanes].astype(F32) * used_col
            g_out[rows, :] = grad.astype(BF16)
            delta = jnp.sum(jnp.transpose(grad * o_buf[i, :, lanes].astype(F32)), axis=0, keepdims=True)
            high = delta.astype(BF16)
            low = (delta - high.astype(F32)).astype(BF16)
            g_out[QROWS + h : QROWS + h + 1, :] = high
            g_out[QROWS + 16 + h : QROWS + 17 + h, :] = low


def wide(row):
    return jnp.concatenate([row] * GROUP, axis=1)


def nt(a, b):
    return lax.dot_general(a, b, (((1,), (1,)), ((), ())), preferred_element_type=F32)


def tn(a, b):
    return lax.dot_general(a, b, (((0,), (0,)), ((), ())), preferred_element_type=F32)


def triangle():
    u = lax.broadcasted_iota(jnp.int32, (SHARD, SHARD), 0)
    t = lax.broadcasted_iota(jnp.int32, (SHARD, SHARD), 1)
    return wide(u <= t)


def sides(z, y):
    return (2 * z + y, 2 * z + 1 - y)


def total_step(kv_part, diagonal, key_z, z, y, first_ref, queries, m_ref, l_ref, sources=(0, 1)):
    key_sides = sides(key_z, y)
    query_sides = sides(z, y)
    for src in sources:
        first = first_ref[src : src + 1, :]
        ok = [wide((first <= s) & (s <= query_sides[src])) for s in key_sides]
        for j in range(HALF):
            unit = src * HALF + j
            s = nt(kv_part[j], queries[src][j * UNIT : (j + 1) * UNIT, :]) * SCORE
            parts = [s[:SHARD], s[SHARD:]]
            if diagonal:
                parts[src] = jnp.where(triangle(), parts[src], NEG)
            m = m_ref[unit : unit + 1, :]
            new = m
            for part, good in zip(parts, ok):
                new = jnp.maximum(new, jnp.where(good, jnp.max(part, axis=0, keepdims=True), NEG))
            l = l_ref[unit : unit + 1, :] * jnp.exp2(m - new)
            for part, good in zip(parts, ok):
                l = l + jnp.sum(jnp.exp2(part - jnp.where(good, new, BIG)), axis=0, keepdims=True)
            m_ref[unit : unit + 1, :] = new
            l_ref[unit : unit + 1, :] = l


def keys_of(kv):
    return [kv[:, i * HD : (i + 1) * HD] for i in range(HALF)], [
        kv[:, (HALF + i) * HD : (HALF + i + 1) * HD] for i in range(HALF)
    ]


def totals_kernel(first_call, jobs, *refs):
    meta, first_ref, q_own, q_par = refs[:4]
    n = len(jobs)
    kvs = refs[4 : 4 + n]
    refs = refs[4 + n :]
    if not first_call:
        m_in, l_in = refs[:2]
        refs = refs[2:]
    m_ref, l_ref = refs
    z, y = meta[0], meta[1]
    if first_call:
        m_ref[...] = jnp.full(m_ref.shape, NEG, F32)
        l_ref[...] = jnp.zeros(l_ref.shape, F32)
    else:
        m_ref[...] = m_in[...]
        l_ref[...] = l_in[...]
    for (offset, sources), kv in zip(jobs, kvs):

        @pl.when(z >= offset)
        def _():
            keys, _ = keys_of(kv)
            total_step(keys, offset == 0, z - offset, z, y, first_ref, (q_own, q_par), m_ref, l_ref, sources)


def grads_kernel(offsets, last_total, first_call, final, *refs):
    meta, first_ref, q_own, q_par, g_own, g_par = refs[:6]
    refs = refs[6:]
    n = len(offsets)
    kvs = refs[:n]
    refs = refs[n:]
    if first_call:
        m_in, l_in, count_in = refs[:3]
        refs = refs[3:]
    else:
        lse_in, dq_in = refs[:2]
        refs = refs[2:]
    parts = refs[:n]
    refs = refs[n:]
    if first_call:
        lse_ref, dq_ref, m_ref, l_ref = refs
    elif final:
        dq_own, dq_par, dq_ref = refs
        lse_ref = lse_in
    else:
        (dq_ref,) = refs
        lse_ref = lse_in
    z, y = meta[0], meta[1]
    queries, grads = (q_own, q_par), (g_own, g_par)
    query_sides = sides(z, y)
    if first_call:
        m_ref[...] = m_in[...]
        l_ref[...] = l_in[...]

        @pl.when(z >= last_total)
        def _():
            keys, _ = keys_of(kvs[0])
            total_step(keys, False, z - last_total, z, y, first_ref, queries, m_ref, l_ref)

        total = l_ref[...]
        lse_ref[...] = jnp.where(total > 0.0, m_ref[...] + jnp.log2(jnp.where(total > 0.0, total, 1.0)), BIG)
        dq_ref[...] = jnp.zeros(dq_ref.shape, F32)
    else:
        dq_ref[...] = dq_in[...]
    tail = jnp.zeros((TAIL, 4 * HD), F32)
    if first_call:
        lane = lax.broadcasted_iota(jnp.int32, tail.shape, 1)
        for i in range(2):
            value = jnp.broadcast_to(count_in[:1, i : i + 1], (1, 4 * HD))
            high = value.astype(BF16).astype(F32)
            tail = jnp.where(lane == i, high, jnp.where(lane == 2 + i, value - high, tail))
    for offset, kv, part in zip(offsets, kvs, parts):
        part[2 * SHARD :, :] = tail.astype(part.dtype)

        @pl.when(z < offset)
        def _():
            part[: 2 * SHARD, :] = jnp.zeros((2 * SHARD, 4 * HD), part.dtype)

        @pl.when(z >= offset)
        def _():
            keys, values = keys_of(kv)
            key_sides = sides(z - offset, y)
            for j in range(HALF):
                grad_k = jnp.zeros((2 * SHARD, HD), F32)
                grad_v = jnp.zeros((2 * SHARD, HD), F32)
                for src in range(2):
                    unit = src * HALF + j
                    rows = slice(j * UNIT, (j + 1) * UNIT)
                    first = first_ref[src : src + 1, :]
                    lse = lse_ref[unit : unit + 1, :]
                    query = queries[src][rows, :]
                    grad = grads[src][rows, :]
                    heads = range(j * GROUP, (j + 1) * GROUP)
                    delta = jnp.concatenate(
                        [
                            grads[src][QROWS + h : QROWS + h + 1, :].astype(F32)
                            + grads[src][QROWS + 16 + h : QROWS + 17 + h, :].astype(F32)
                            for h in heads
                        ],
                        axis=1,
                    )
                    s = nt(keys[j], query) * SCORE
                    probs = []
                    for half in range(2):
                        good = wide((first <= key_sides[half]) & (key_sides[half] <= query_sides[src]))
                        p = jnp.exp2(s[half * SHARD : (half + 1) * SHARD] - jnp.where(good, lse, BIG))
                        if offset == 0 and half == src:
                            p = jnp.where(triangle(), p, 0.0)
                        probs.append(p)
                    prob = jnp.concatenate(probs, axis=0)
                    grad_v = grad_v + jnp.dot(prob.astype(BF16), grad, preferred_element_type=F32)
                    dscore = (prob * (nt(values[j], grad) - delta)).astype(BF16)
                    grad_k = grad_k + jnp.dot(dscore, query, preferred_element_type=F32)
                    dq_ref[unit] += tn(keys[j], dscore)
                part[: 2 * SHARD, j * HD : (j + 1) * HD] = (grad_k * INV).astype(part.dtype)
                part[: 2 * SHARD, (HALF + j) * HD : (HALF + j + 1) * HD] = grad_v.astype(part.dtype)

    if final:
        for src, out in enumerate((dq_own, dq_par)):
            for h in range(QH):
                j, g = divmod(h, GROUP)
                block = dq_ref[src * HALF + j, :, g * SHARD : (g + 1) * SHARD]
                out[:, h * HD : (h + 1) * HD] = (jnp.transpose(block) * INV).astype(BF16)


def finish_kernel(meta, dq_own, dq_back, kv_own, kv_back, count, moved, grad_query, grad_key, grad_value):
    y = meta[1]
    present, marked = (count[:1, i : i + 1] + moved[:1, i : i + 1] + moved[:1, 2 + i : 3 + i] for i in range(2))
    scale = jnp.broadcast_to(present / marked, (1, HD))
    for mine, dq, kv in ((True, dq_own, kv_own), (False, dq_back, kv_back)):
        side = y if mine else 1 - y
        for h in range(QH):
            lanes = pl.ds(pl.multiple_of(side * (QH * HD) + h * HD, HD), HD)
            grad_query[:, lanes] = (dq[:, h * HD : (h + 1) * HD].astype(F32) * scale).astype(BF16)
        for j in range(HALF):
            lanes = pl.ds(pl.multiple_of((side * HALF + j) * HD, HD), HD)
            grad_key[:, lanes] = (kv[:, j * HD : (j + 1) * HD].astype(F32) * scale).astype(BF16)
            value = kv[:, (HALF + j) * HD : (HALF + j + 1) * HD].astype(F32) * scale
            grad_value[:, lanes] = value.astype(BF16)


def per_device(query_rows, key_rows, value_rows, forward_out, out_grad, lengths, starts, adv_mask):
    here = lax.axis_index("ctx")
    z, y = here // 2, here % 2
    meta = jnp.stack([z, y]).astype(jnp.int32)
    rows_dp = lax.axis_size("dp")

    def along(value, steps, sources, flip=0):
        pairs = [(2 * s + w, 2 * ((s + steps) % RING) + (w ^ flip)) for s in sources for w in range(2)]
        return lax.ppermute(value, "ctx", pairs)

    def across(value):
        return lax.ppermute(value, "ctx", [(i, i ^ 1) for i in range(2 * RING)])

    kv_shape = ((SHARD, 4 * HD), BF16)
    q_shape = ((QROWS, HD), BF16)
    g_shape = ((QROWS + 32, HD), BF16)
    kv_keep, kv_send, first, used, count = call(
        keys_kernel,
        [kv_shape, kv_shape, ((8, SHARD), jnp.int32), ((8, SHARD), F32), ((8, HD), F32)],
        (meta, *map(in_hbm, (lengths, starts, adv_mask, key_rows[0], value_rows[0]))),
        [SMEM] + [HBM] * 5,
        scratch_shapes=[
            pltpu.SMEM((1, 4), jnp.int32),
            pltpu.SMEM((1, 4), jnp.int32),
            pltpu.VMEM((1, SHARD), jnp.int32),
            pltpu.SemaphoreType.DMA((7,)),
        ],
    )
    q_own, q_send, g_own, g_send = call(
        queries_kernel,
        [q_shape, q_shape, g_shape, g_shape],
        (meta, used, *map(in_hbm, (query_rows[0], forward_out[0], out_grad[0]))),
        [SMEM, VMEM] + [HBM] * 3,
        flops=1 << 28,
        scratch_shapes=[pltpu.VMEM((2, SHARD, QH * HD), BF16)] * 3 + [pltpu.SemaphoreType.DMA((6,))],
    )

    everyone = range(RING)
    ahead = jnp.concatenate([along(kv_keep, 1, everyone), along(kv_send, 1, everyone, 1)], axis=0)
    back = jnp.concatenate([along(kv_keep, -1, everyone), along(kv_send, -1, everyone, 1)], axis=0)
    held = {0: jnp.concatenate([kv_keep, across(kv_send)], axis=0), 1: ahead, RING - 1: back}
    q_par = across(q_send)
    g_par = across(g_send)

    def counted(count, bit):
        if bit >= rows_dp:
            return count
        flip = 1 if bit == 2 else 0
        pairs = [((i ^ bit) * 2 * RING + (j ^ flip), i * 2 * RING + j) for i in range(rows_dp) for j in range(2 * RING)]
        return count + lax.ppermute(count, ("dp", "ctx"), pairs)

    state = [((2 * HALF, UNIT), F32)] * 2

    def totals(jobs, prev):
        return call(
            functools.partial(totals_kernel, prev is None, jobs),
            state,
            (meta, first, q_own, q_par if any(1 in w for _, w in jobs) else q_own, *[held[i] for i, _ in jobs], *(prev or ())),
            [SMEM],
            flops=4 * unit_flops * len(jobs),
        )

    unit_flops = 2 * 256 * UNIT * HD * 4
    own, par, both = (0,), (1,), (0, 1)
    count = counted(count + across(count), 2)
    ahead, count = lax.optimization_barrier((ahead, count))
    held[2] = ahead = along(ahead, 1, everyone)
    held[6] = back = along(back, -1, everyone)
    ml = totals(((1, own), (7, own)), None)
    count = counted(count, 1)
    ahead, ml, count = lax.optimization_barrier((ahead, ml, count))
    held[3] = ahead = along(ahead, 1, everyone)
    held[5] = back = along(back, -1, everyone)
    ml = totals(((2, own), (6, own)), ml)
    count = counted(counted(count, 4), 8)
    ahead, ml, count = lax.optimization_barrier((ahead, ml, count))
    held[4] = along(ahead, 1, everyone)
    ml = totals(((0, both), (1, par), (7, par), (2, par), (6, par)), ml)
    ml = totals(((3, both), (5, both)), ml)

    dq_shape = ((2 * HALF, HD, UNIT), F32)
    part_shape = (2 * SHARD + TAIL, 4 * HD)
    common = (meta, first, q_own, q_par, g_own, g_par)

    def grads(offsets, extra, outs, first_call=False, final=False, kind=F32, **kw):
        return call(
            functools.partial(grads_kernel, offsets, 4, first_call, final),
            [(part_shape, kind)] * len(offsets) + outs,
            (*common, *[held[i] for i in offsets], *extra),
            [SMEM],
            flops=8 * unit_flops * len(offsets),
            **kw,
        )

    def add(moved, part):
        return (moved.astype(F32) + part).astype(BF16)

    part4, part5, lse, dq = grads(
        (4, 5),
        (*ml, count),
        [((2 * HALF, UNIT), F32), dq_shape],
        first_call=True,
        kind=BF16,
        scratch_shapes=[pltpu.VMEM((2 * HALF, UNIT), F32)] * 2,
    )
    down = [along(part4, -1, everyone)]
    up = [along(part5, 1, everyone)]
    part3, part6, dq = grads((3, 6), (lse, dq), [dq_shape])
    down.append(along(add(down[-1], part3), -1, everyone))
    up.append(along(add(up[-1], part6), 1, everyone))
    part2, part7, dq = grads((2, 7), (lse, dq), [dq_shape])
    down.append(along(add(down[-1], part2), -1, everyone))
    up.append(along(add(up[-1], part7), 1, everyone))
    part1, part0, dq_own, dq_par = grads(
        (1, 0),
        (lse, dq),
        [((SHARD, QH * HD), BF16)] * 2,
        final=True,
        scratch_shapes=[pltpu.VMEM(*dq_shape)],
    )
    dq_back = across(dq_par)
    down.append(along(add(down[-1], part1), -1, everyone))
    total = (part0 + down[-1].astype(F32) + up[-1].astype(F32))[: 2 * SHARD]
    kv_back = across(total[SHARD:].astype(BF16))
    moved = sum(x[2 * SHARD :, :HD].astype(F32) for x in down + up)
    grad_query, grad_key, grad_value = call(
        finish_kernel,
        [((SHARD, KVH * GROUP * HD), BF16), ((SHARD, KVH * HD), BF16), ((SHARD, KVH * HD), BF16)],
        (meta, dq_own, dq_back, total[:SHARD], kv_back, count, moved),
        [SMEM],
    )
    return grad_query[None], grad_key[None], grad_value[None]


def solution(mesh):
    in_specs = (
        P("dp", "ctx", None),
        P("dp", "ctx", None),
        P("dp", "ctx", None),
        P("dp", "ctx", None),
        P("dp", "ctx", None),
        P("dp", None),
        P("dp", None),
        P("dp", "ctx"),
    )
    out_specs = (P("dp", "ctx", None), P("dp", "ctx", None), P("dp", "ctx", None))
    return jax.shard_map(
        per_device, mesh=mesh, in_specs=in_specs, out_specs=out_specs, check_vma=False
    )
```

```python
import functools
import math

import jax
import jax.numpy as jnp
from jax import lax
from jax.experimental import pallas as pl
from jax.experimental.pallas import tpu as pltpu
from jax.sharding import PartitionSpec as P

KVH = 4
GROUP = 5
HD = 128
SHARD = 128
RING = 8
HALF = KVH // 2
QH = HALF * GROUP
QROWS = QH * SHARD
UNIT = GROUP * SHARD
TAIL = 16
NEG = -1e30
BIG = 1e30
SCORE = math.log2(math.e) / math.sqrt(HD)
INV = 1.0 / math.sqrt(HD)
F32 = jnp.float32
BF16 = jnp.bfloat16
VMEM = pl.BlockSpec(memory_space=pltpu.VMEM)
SMEM = pl.BlockSpec(memory_space=pltpu.SMEM)
HBM = pl.BlockSpec(memory_space=pltpu.HBM)
DEAD = 1 << 20
LIMIT = 48 * 1024 * 1024


def call(body, outs, ins, specs, flops=0, **kw):
    return pl.pallas_call(
        body,
        out_shape=[jax.ShapeDtypeStruct(s, d) for s, d in outs],
        in_specs=list(specs) + [VMEM] * (len(ins) - len(specs)),
        out_specs=[VMEM] * len(outs),
        compiler_params=pltpu.CompilerParams(vmem_limit_bytes=LIMIT),
        cost_estimate=pl.CostEstimate(flops=flops, bytes_accessed=4 << 20, transcendentals=0),
        **kw,
    )(*ins)


def in_hbm(value):
    return pltpu.with_memory_space_constraint(value, pltpu.HBM)


def fetch(copies, sems):
    started = [pltpu.make_async_copy(a, b, sems.at[i]) for i, (a, b) in enumerate(copies)]
    for one in started:
        one.start()
    return started


def half_lanes(side, width):
    return pl.ds(pl.multiple_of(side * width, width), width)


def keys_kernel(meta, len_hbm, start_hbm, adv_hbm, k, v, kv_keep, kv_send, first_ref, used_ref, count_ref, lens, begins, adv, sems):
    z, y = meta[0], meta[1]
    width = HALF * HD
    copies = [(len_hbm, lens), (start_hbm, begins), (adv_hbm, adv)]
    for side, out in ((y, kv_keep), (1 - y, kv_send)):
        copies.append((k.at[:, half_lanes(side, width)], out.at[:, :width]))
        copies.append((v.at[:, half_lanes(side, width)], out.at[:, width:]))
    started = fetch(copies, sems)
    for one in started[:3]:
        one.wait()
    for i, shard in enumerate(sides(z, y)):
        tok = shard * SHARD + lax.broadcasted_iota(jnp.int32, (1, SHARD), 1)
        first = jnp.full((1, SHARD), DEAD, jnp.int32)
        for r in range(4):
            begin = begins[0, r] * SHARD
            first = jnp.where((tok >= begin) & (tok < begin + lens[0, r]), begins[0, r], first)
        first_ref[i : i + 1, :] = first
    live = (first_ref[:1, :] < DEAD).astype(F32)
    used = live * adv[...].astype(F32)
    used_ref[...] = jnp.broadcast_to(used, used_ref.shape)
    present = jnp.sum(live, axis=1, keepdims=True)
    marked = jnp.sum(used, axis=1, keepdims=True)
    lane = lax.broadcasted_iota(jnp.int32, count_ref.shape, 1)
    count_ref[...] = jnp.where(lane == 0, present, jnp.where(lane == 1, marked, 0.0))
    for one in started[3:]:
        one.wait()


def queries_kernel(meta, used, q, o, og, q_keep, q_send, g_keep, g_send, q_buf, o_buf, og_buf, sems):
    y = meta[1]
    width = QH * HD
    copies = []
    for i, side in ((1, 1 - y), (0, y)):
        for whole, buf in ((q, q_buf), (og, og_buf), (o, o_buf)):
            copies.append((whole.at[:, half_lanes(side, width)], buf.at[i]))
    started = fetch(copies, sems)
    used_col = jnp.transpose(jnp.broadcast_to(used[:1, :], (SHARD, SHARD)))
    for n, (i, q_out, g_out) in enumerate(((1, q_send, g_send), (0, q_keep, g_keep))):
        for one in started[3 * n : 3 * n + 3]:
            one.wait()
        for h in range(QH):
            lanes = slice(h * HD, (h + 1) * HD)
            rows = slice(h * SHARD, (h + 1) * SHARD)
            q_out[rows, :] = q_buf[i, :, lanes]
            grad = og_buf[i, :, lanes].astype(F32) * used_col
            g_out[rows, :] = grad.astype(BF16)
            delta = jnp.sum(jnp.transpose(grad * o_buf[i, :, lanes].astype(F32)), axis=0, keepdims=True)
            high = delta.astype(BF16)
            low = (delta - high.astype(F32)).astype(BF16)
            g_out[QROWS + h : QROWS + h + 1, :] = high
            g_out[QROWS + 16 + h : QROWS + 17 + h, :] = low


def wide(row):
    return jnp.concatenate([row] * GROUP, axis=1)


def nt(a, b):
    return lax.dot_general(a, b, (((1,), (1,)), ((), ())), preferred_element_type=F32)


def tn(a, b):
    return lax.dot_general(a, b, (((0,), (0,)), ((), ())), preferred_element_type=F32)


def triangle():
    u = lax.broadcasted_iota(jnp.int32, (SHARD, SHARD), 0)
    t = lax.broadcasted_iota(jnp.int32, (SHARD, SHARD), 1)
    return wide(u <= t)


def sides(z, y):
    return (2 * z + y, 2 * z + 1 - y)


def total_step(kv_part, diagonal, key_z, z, y, first_ref, queries, m_ref, l_ref, sources=(0, 1)):
    key_sides = sides(key_z, y)
    query_sides = sides(z, y)
    for src in sources:
        first = first_ref[src : src + 1, :]
        ok = [wide((first <= s) & (s <= query_sides[src])) for s in key_sides]
        for j in range(HALF):
            unit = src * HALF + j
            s = nt(kv_part[j], queries[src][j * UNIT : (j + 1) * UNIT, :]) * SCORE
            parts = [s[:SHARD], s[SHARD:]]
            if diagonal:
                parts[src] = jnp.where(triangle(), parts[src], NEG)
            m = m_ref[unit : unit + 1, :]
            new = m
            for part, good in zip(parts, ok):
                new = jnp.maximum(new, jnp.where(good, jnp.max(part, axis=0, keepdims=True), NEG))
            l = l_ref[unit : unit + 1, :] * jnp.exp2(m - new)
            for part, good in zip(parts, ok):
                l = l + jnp.sum(jnp.exp2(part - jnp.where(good, new, BIG)), axis=0, keepdims=True)
            m_ref[unit : unit + 1, :] = new
            l_ref[unit : unit + 1, :] = l


def keys_of(kv):
    return [kv[: 2 * SHARD, i * HD : (i + 1) * HD] for i in range(HALF)], [
        kv[: 2 * SHARD, (HALF + i) * HD : (HALF + i + 1) * HD] for i in range(HALF)
    ]


def totals_kernel(first_call, jobs, *refs):
    meta, first_ref, q_own, q_par = refs[:4]
    n = len(jobs)
    kvs = refs[4 : 4 + n]
    refs = refs[4 + n :]
    if not first_call:
        m_in, l_in = refs[:2]
        refs = refs[2:]
    m_ref, l_ref = refs
    z, y = meta[0], meta[1]
    if first_call:
        m_ref[...] = jnp.full(m_ref.shape, NEG, F32)
        l_ref[...] = jnp.zeros(l_ref.shape, F32)
    else:
        m_ref[...] = m_in[...]
        l_ref[...] = l_in[...]
    for (offset, sources), kv in zip(jobs, kvs):

        @pl.when(z >= offset)
        def _():
            keys, _ = keys_of(kv)
            total_step(keys, offset == 0, z - offset, z, y, first_ref, (q_own, q_par), m_ref, l_ref, sources)


def chunk_grads(group, z, y, first_ref, lse_ref, queries, grads, dq_ref):
    query_sides = sides(z, y)
    blocks = [(offset, half) for offset, _, _ in group for half in range(2)]
    loaded = [keys_of(kv) for _, kv, _ in group]
    for j in range(HALF):
        keys, values = (jnp.concatenate([one[i][j] for one in loaded], axis=0) for i in range(2))
        grad_k = grad_v = jnp.zeros((len(blocks) * SHARD, HD), F32)
        for src in range(2):
            unit = src * HALF + j
            rows = slice(j * UNIT, (j + 1) * UNIT)
            first = first_ref[src : src + 1, :]
            lse = lse_ref[unit : unit + 1, :]
            query = queries[src][rows, :]
            grad = grads[src][rows, :]
            delta = jnp.concatenate(
                [
                    grads[src][QROWS + h : QROWS + h + 1, :].astype(F32)
                    + grads[src][QROWS + 16 + h : QROWS + 17 + h, :].astype(F32)
                    for h in range(j * GROUP, (j + 1) * GROUP)
                ],
                axis=1,
            )
            s = nt(keys, query) * SCORE
            probs = []
            for i, (offset, half) in enumerate(blocks):
                shard = sides(z - offset, y)[half]
                good = wide((first <= shard) & (shard <= query_sides[src]))
                p = jnp.exp2(s[i * SHARD : (i + 1) * SHARD] - jnp.where(good, lse, BIG))
                if offset == 0 and half == src:
                    p = jnp.where(triangle(), p, 0.0)
                probs.append(p)
            prob = jnp.concatenate(probs, axis=0)
            grad_v = grad_v + jnp.dot(prob.astype(BF16), grad, preferred_element_type=F32)
            dscore = (prob * (nt(values, grad) - delta)).astype(BF16)
            grad_k = grad_k + jnp.dot(dscore, query, preferred_element_type=F32)
            dq_ref[unit] += tn(keys, dscore)
        for i, (_, _, part) in enumerate(group):
            rows = slice(2 * SHARD * i, 2 * SHARD * (i + 1))
            part[: 2 * SHARD, j * HD : (j + 1) * HD] = (grad_k[rows] * INV).astype(part.dtype)
            part[: 2 * SHARD, (HALF + j) * HD : (HALF + j + 1) * HD] = grad_v[rows].astype(part.dtype)


def grads_kernel(offsets, first_call, final, *refs):
    meta, tail_in, first_ref, q_own, q_par, g_own, g_par = refs[:7]
    kvs, refs = refs[7:9], refs[9:]
    if first_call:
        m_in, l_in, *parts, lse_ref, dq_ref, m_ref, l_ref = refs
    elif final:
        lse_ref, dq_in, *parts, dq_own, dq_par, dq_ref = refs
    else:
        lse_ref, dq_in, *parts, dq_ref = refs
    z, y = meta[0], meta[1]
    queries, grads = (q_own, q_par), (g_own, g_par)
    if first_call:
        m_ref[...] = m_in[...]
        l_ref[...] = l_in[...]

        @pl.when(z >= offsets[0])
        def _():
            keys, _ = keys_of(kvs[0])
            total_step(keys, False, z - offsets[0], z, y, first_ref, queries, m_ref, l_ref)

        total = l_ref[...]
        lse_ref[...] = jnp.where(total > 0.0, m_ref[...] + jnp.log2(jnp.where(total > 0.0, total, 1.0)), BIG)
        dq_ref[...] = jnp.zeros(dq_ref.shape, F32)
    else:
        dq_ref[...] = dq_in[...]
    far, near = sorted(range(2), key=lambda i: -offsets[i])
    tails = (tail_in[...], kvs[0][2 * SHARD :, :]) if first_call else (jnp.zeros((TAIL, 4 * HD), F32),) * 2
    for i in range(2):
        parts[i][2 * SHARD :, :] = tails[i].astype(parts[i].dtype)

        @pl.when(z < offsets[i])
        def _():
            parts[i][: 2 * SHARD, :] = jnp.zeros((2 * SHARD, 4 * HD), parts[i].dtype)

    def run(which):
        group = [(offsets[i], kvs[i], parts[i]) for i in which]
        chunk_grads(group, z, y, first_ref, lse_ref, queries, grads, dq_ref)

    @pl.when(z >= offsets[far])
    def _():
        run((far, near))

    @pl.when((z >= offsets[near]) & (z < offsets[far]))
    def _():
        run((near,))

    if final:
        for src, out in enumerate((dq_own, dq_par)):
            for h in range(QH):
                j, g = divmod(h, GROUP)
                block = dq_ref[src * HALF + j, :, g * SHARD : (g + 1) * SHARD]
                out[:, h * HD : (h + 1) * HD] = (jnp.transpose(block) * INV).astype(BF16)


def finish_kernel(meta, dq_own, dq_back, kv_own, kv_back, count, grad_query, grad_key, grad_value):
    y = meta[1]
    present, marked = (count[:1, i : i + 1] + count[:1, 2 + i : 3 + i] for i in range(2))
    scale = jnp.broadcast_to(present / marked, (1, HD))
    for mine, dq, kv in ((True, dq_own, kv_own), (False, dq_back, kv_back)):
        side = y if mine else 1 - y
        for h in range(QH):
            lanes = pl.ds(pl.multiple_of(side * (QH * HD) + h * HD, HD), HD)
            grad_query[:, lanes] = (dq[:, h * HD : (h + 1) * HD].astype(F32) * scale).astype(BF16)
        for j in range(HALF):
            lanes = pl.ds(pl.multiple_of((side * HALF + j) * HD, HD), HD)
            grad_key[:, lanes] = (kv[:, j * HD : (j + 1) * HD].astype(F32) * scale).astype(BF16)
            value = kv[:, (HALF + j) * HD : (HALF + j + 1) * HD].astype(F32) * scale
            grad_value[:, lanes] = value.astype(BF16)


def per_device(query_rows, key_rows, value_rows, forward_out, out_grad, lengths, starts, adv_mask):
    here = lax.axis_index("ctx")
    z, y = here // 2, here % 2
    meta = jnp.stack([z, y]).astype(jnp.int32)
    rows_dp = lax.axis_size("dp")

    def along(value, steps, sources, flip=0):
        pairs = [(2 * s + w, 2 * ((s + steps) % RING) + (w ^ flip)) for s in sources for w in range(2)]
        return lax.ppermute(value, "ctx", pairs)

    def across(value):
        return lax.ppermute(value, "ctx", [(i, i ^ 1) for i in range(2 * RING)])

    kv_shape = ((SHARD, 4 * HD), BF16)
    q_shape = ((QROWS, HD), BF16)
    g_shape = ((QROWS + 32, HD), BF16)
    kv_keep, kv_send, first, used, count = call(
        keys_kernel,
        [kv_shape, kv_shape, ((8, SHARD), jnp.int32), ((8, SHARD), F32), ((8, HD), F32)],
        (meta, *map(in_hbm, (lengths, starts, adv_mask, key_rows[0], value_rows[0]))),
        [SMEM] + [HBM] * 5,
        scratch_shapes=[
            pltpu.SMEM((1, 4), jnp.int32),
            pltpu.SMEM((1, 4), jnp.int32),
            pltpu.VMEM((1, SHARD), jnp.int32),
            pltpu.SemaphoreType.DMA((7,)),
        ],
    )
    q_own, q_send, g_own, g_send = call(
        queries_kernel,
        [q_shape, q_shape, g_shape, g_shape],
        (meta, used, *map(in_hbm, (query_rows[0], forward_out[0], out_grad[0]))),
        [SMEM, VMEM] + [HBM] * 3,
        flops=1 << 28,
        scratch_shapes=[pltpu.VMEM((2, SHARD, QH * HD), BF16)] * 3 + [pltpu.SemaphoreType.DMA((6,))],
    )

    everyone = range(RING)

    ahead = jnp.concatenate([along(kv_keep, 1, everyone), along(kv_send, 1, everyone, 1)], axis=0)
    back = jnp.concatenate([along(kv_keep, -1, everyone), along(kv_send, -1, everyone, 1)], axis=0)
    held = {0: jnp.concatenate([kv_keep, across(kv_send)], axis=0), 1: ahead, RING - 1: back}
    q_par = across(q_send)
    g_par = across(g_send)

    def counted(count, bits):
        total = count
        for bit in bits:
            if bit < rows_dp:
                flip = 1 if bit == 2 else 0
                pairs = [
                    ((i ^ bit) * 2 * RING + (j ^ flip), i * 2 * RING + j) for i in range(rows_dp) for j in range(2 * RING)
                ]
                total = total + lax.ppermute(count, ("dp", "ctx"), pairs)
        return total

    state = [((2 * HALF, UNIT), F32)] * 2

    def totals(jobs, prev):
        return call(
            functools.partial(totals_kernel, prev is None, jobs),
            state,
            (meta, first, q_own, q_par if any(1 in w for _, w in jobs) else q_own, *[held[i] for i, _ in jobs], *(prev or ())),
            [SMEM],
            flops=4 * unit_flops * len(jobs),
        )

    unit_flops = 2 * 256 * UNIT * HD * 4
    own, par, both = (0,), (1,), (0, 1)
    count = counted(count + across(count), (2,))
    ahead, count = lax.optimization_barrier((ahead, count))
    held[2] = ahead = along(ahead, 1, everyone)
    held[6] = back = along(back, -1, everyone)
    ml = totals(((1, own), (7, own)), None)
    ahead, ml = lax.optimization_barrier((ahead, ml))
    held[3] = ahead = along(ahead, 1, everyone)
    held[5] = back = along(back, -1, everyone)
    ml = totals(((2, own), (6, own)), ml)
    count = counted(count, (1,))
    ahead, ml, count = lax.optimization_barrier((ahead, ml, count))
    high = jnp.floor(count[:, :2] / 64.0) * 64.0
    tail = jnp.concatenate([high, count[:, :2] - high, jnp.zeros((8, 4 * HD - 4), F32)], axis=1)
    tail = jnp.concatenate([tail, tail], axis=0).astype(BF16)
    held[4] = along(jnp.concatenate([ahead, tail], axis=0), 1, everyone)
    ml = totals(((0, both), (1, par), (7, par), (2, par), (6, par)), ml)
    ml = totals(((3, both), (5, both)), ml)

    dq_shape = ((2 * HALF, HD, UNIT), F32)
    part_shape = (2 * SHARD + TAIL, 4 * HD)
    common = (meta, tail, first, q_own, q_par, g_own, g_par)

    def grads(offsets, extra, outs, first_call=False, final=False, kinds=(F32, F32), **kw):
        return call(
            functools.partial(grads_kernel, offsets, first_call, final),
            [(part_shape, kind) for kind in kinds] + outs,
            (*common, *[held[i] for i in offsets], *extra),
            [SMEM],
            flops=16 * unit_flops,
            **kw,
        )

    def add(moved, part):
        return (moved.astype(F32) + part).astype(BF16)

    part4, part5, lse, dq = grads(
        (4, 5),
        ml,
        [((2 * HALF, UNIT), F32), dq_shape],
        first_call=True,
        kinds=(BF16, BF16),
        scratch_shapes=[pltpu.VMEM((2 * HALF, UNIT), F32)] * 2,
    )
    down = [along(part4, -1, everyone)]
    up = [along(part5, 1, everyone)]
    for offsets in ((3, 6), (2, 7)):
        for_down, for_up, dq = grads(offsets, (lse, dq), [dq_shape])
        sums = lax.optimization_barrier((add(down[-1], for_down), add(up[-1], for_up)))
        down.append(along(sums[0], -1, everyone))
        up.append(along(sums[1], 1, everyone))
    part1, part0, dq_own, dq_par = grads(
        (1, 0),
        (lse, dq),
        [((SHARD, QH * HD), BF16)] * 2,
        final=True,
        scratch_shapes=[pltpu.VMEM(*dq_shape)],
    )
    dq_back = across(dq_par)
    last, up[-1] = lax.optimization_barrier((add(down[-1], part1), up[-1]))
    down.append(along(last, -1, everyone))
    total = (part0 + down[-1].astype(F32) + up[-1].astype(F32))[: 2 * SHARD]
    kv_back = across(total[SHARD:].astype(BF16))
    moved = sum(x[2 * SHARD : 2 * SHARD + 8, :HD].astype(F32) for x in [held[4], *down[:3], *up])
    count = counted(count + moved, (4, 8, 12))
    grad_query, grad_key, grad_value = call(
        finish_kernel,
        [((SHARD, KVH * GROUP * HD), BF16), ((SHARD, KVH * HD), BF16), ((SHARD, KVH * HD), BF16)],
        (meta, dq_own, dq_back, total[:SHARD], kv_back, count),
        [SMEM],
    )
    return grad_query[None], grad_key[None], grad_value[None]


def solution(mesh):
    in_specs = (
        P("dp", "ctx", None),
        P("dp", "ctx", None),
        P("dp", "ctx", None),
        P("dp", "ctx", None),
        P("dp", "ctx", None),
        P("dp", None),
        P("dp", None),
        P("dp", "ctx"),
    )
    out_specs = (P("dp", "ctx", None), P("dp", "ctx", None), P("dp", "ctx", None))
    return jax.shard_map(
        per_device, mesh=mesh, in_specs=in_specs, out_specs=out_specs, check_vma=False
    )
```
